768 devices in a mesh: blk: 384 (over x, y, z), grp: 2 (over core).
Axes of the slice: x: 4, y: 8, z: 12, core: 2. Of those that a mesh axis runs over, the one named last changes fastest.
Arguments:
- item_factors: bfloat16 [12288, 256], P(('blk', 'grp')), may hold values from -0.0546875 to 0.0546875
- user_start: float32 [98304, 256], P('blk'), may hold values from -6 to 6
- tile_items: int32 [384, 48], P('blk'), may hold values from 0 to 47, as said below
- tile_count: int32 [384], P('blk'), may hold values from 1 to 48, as said below
- tile_seed: int32 [384, 48], P('blk'), may hold values from 0 to 65520
Outputs:
- solution: float32 [98304, 256], P('blk', 'grp')
- residual: float32 [98304, 256], P('blk', 'grp')
The draws below stay inside these ranges and needn't reach their ends.
Inputs may be any that keep to these rules, and one draw needn't show every extreme that they name: `tile_items`: each row is a permutation of the 48 item blocks. `tile_count`: skewed toward few heavy user blocks; some user block has all 48 slots live.
All inputs are finite; a program needn't handle non-finite values.
Results may differ from the reference program's by a relative error of at most 0.0095.
Values may be sent and summed in bfloat16 or wider, within the bound.
A program may use at most 64 MiB of HBM per device.

```python
import jax
import jax.numpy as jnp
from jax import lax

RANK = 256
BLOCK = 256
STEPS = 2
ITEMS = 12288
NIB = 48
UBLOCKS = 384
USERS = 98304


def draw_tile_count(key, part):
    key = jax.random.fold_in(key, 11)
    first_key, second_key = jax.random.split(key)
    picked = jax.random.randint(first_key, (UBLOCKS,), 0, NIB)
    counts = 1 + picked * picked * picked // (NIB * NIB)
    heavy_row = jax.random.randint(second_key, (), 0, UBLOCKS)
    positions = jnp.arange(UBLOCKS, dtype=jnp.int32)
    counts = jnp.where(positions == heavy_row, NIB, counts)
    return jnp.minimum(counts, NIB).astype(jnp.int32)


def draw_tile_items(key, part):
    key = jax.random.fold_in(key, 12)
    scores = jax.random.randint(key, (UBLOCKS, NIB), 0, 1 << 20) * NIB
    scores = scores + jnp.arange(NIB, dtype=jnp.int32)[None, :]
    return jnp.argsort(scores, axis=1, stable=True).astype(jnp.int32)


def place_ends(values, key, low, top_value):
    index_at = [jax.random.randint(jax.random.fold_in(key, axis), (), 0, length) for axis, length in enumerate(values.shape)]
    widest = values.shape.index(max(values.shape))
    beside = index_at[:widest] + [(index_at[widest] + 1) % values.shape[widest]] + index_at[widest + 1:]
    return values.at[tuple(index_at)].set(low).at[tuple(beside)].set(top_value)


def block_levels(stream_key, dims, pieces, smallest, top_value):
    def one(axis_at, blocks):
        heights = jax.random.uniform(jax.random.fold_in(jax.random.fold_in(stream_key, 6), axis_at), (blocks,), jnp.float32, smallest / len(pieces), top_value / len(pieces))
        return jnp.repeat(jnp.exp(heights), dims[axis_at] // blocks).reshape((-1,) + (1,) * (len(dims) - axis_at - 1))

    gain = one(*pieces[0])
    for cut in pieces[1:]:
        gain = gain * one(*cut)
    return gain


def bell_draw(stream_key, extent, deviation, bound, cuts=(), kind=jnp.bfloat16):
    values = deviation * jax.random.normal(stream_key, extent, jnp.float32)
    if cuts:
        values = values * block_levels(stream_key, extent, cuts, -0.22, 0.18)
    return jnp.clip(values, -bound, bound).astype(kind)


def setup_inputs(seed: int = 0) -> dict:
    keys = jax.random.split(jax.random.key(seed), 6)
    return {
        "item_factors": bell_draw(keys[0], (ITEMS, RANK), ITEMS ** -0.5, 0.0546875, ((0, 768),)),
        "user_start": bell_draw(keys[1], (USERS, RANK), 1.0, 6.0, ((0, 384),), jnp.float32),
        "tile_items": draw_tile_items(jax.random.fold_in(keys[5], 71), 0),
        "tile_count": draw_tile_count(jax.random.fold_in(keys[5], 71), 0),
        "tile_seed": place_ends(jax.random.randint(keys[4], (UBLOCKS, NIB), 0, 65521), jax.random.fold_in(keys[4], 1), 0, 65520).astype(jnp.int32),
    }


ridge_weight = 0.5


def tile_pair(tile_seed, tile_width):
    row_ids = lax.broadcasted_iota(jnp.int32, (tile_width, tile_width), 0)
    col_ids = lax.broadcasted_iota(jnp.int32, (tile_width, tile_width), 1)
    hashed = (tile_seed % 65521) * 509 + row_ids * 7883 + col_ids * 6151
    hashed = ((hashed % 65521) * 32749) % 65521
    hashed = (hashed * 32749 + row_ids * 31 + col_ids * 17) % 65521
    observed = (hashed % 2).astype(jnp.float32)
    confidence = observed * (0.5 + 0.0035 * ((hashed // 2) % 1000).astype(jnp.float32))
    return observed, confidence


def tile_term(user_rows, factors, item_index, tile_seed, with_rhs):
    tile_width = user_rows.shape[0]
    item_block = lax.dynamic_slice_in_dim(factors, item_index.astype(jnp.int32) * tile_width, tile_width, 0)
    observed, confidence = tile_pair(tile_seed, tile_width)
    scores = lax.dot_general(user_rows, item_block, (((1,), (1,)), ((), ())), preferred_element_type=jnp.float32)
    weighted = (confidence * scores).astype(jnp.bfloat16)
    result = -jnp.dot(weighted, item_block, preferred_element_type=jnp.float32)
    if with_rhs:
        result = result + jnp.dot((observed + confidence).astype(jnp.bfloat16), item_block, preferred_element_type=jnp.float32)
    return result


def reference_sweep(vector, item_factors, tile_items, tile_count, tile_seed, with_rhs):
    nblocks = vector.shape[0] // BLOCK
    stacked = vector.astype(jnp.bfloat16).reshape(nblocks, BLOCK, vector.shape[1])

    def one_block(packed):
        user_rows, item_row, live_count, seed_row = packed

        def add_slot(slot_index, running):
            slot_index = slot_index.astype(jnp.int32)
            return lax.cond(slot_index < live_count,
                            lambda running_sum: running_sum + tile_term(user_rows, item_factors, item_row[slot_index], seed_row[slot_index], with_rhs),
                            lambda running_sum: running_sum, running)

        return lax.fori_loop(0, item_row.shape[0], add_slot, jnp.zeros(user_rows.shape, jnp.float32))

    return lax.map(one_block, (stacked, tile_items, tile_count, tile_seed)).reshape(vector.shape)


def reference(item_factors, user_start, tile_items, tile_count, tile_seed):
    full_rank = item_factors.shape[1]
    gram_matrix = lax.dot_general(item_factors, item_factors, (((0,), (0,)), ((), ())), preferred_element_type=jnp.float32)
    shifted = gram_matrix + ridge_weight * jnp.eye(full_rank, dtype=jnp.float32)

    def operate(vector):
        return jnp.dot(vector, shifted, precision=lax.Precision.HIGHEST)

    start = reference_sweep(user_start, item_factors, tile_items, tile_count, tile_seed, True)
    residual = start - operate(user_start)
    solution = user_start
    direction = residual
    norm_now = jnp.sum(residual * residual, axis=1, keepdims=True)
    for number in range(STEPS):
        applied = operate(direction) - reference_sweep(direction, item_factors, tile_items, tile_count, tile_seed, False)
        curvature = jnp.sum(direction * applied, axis=1, keepdims=True)
        step_size = norm_now / curvature
        solution = solution + step_size * direction
        residual = residual - step_size * applied
        norm_next = jnp.sum(residual * residual, axis=1, keepdims=True)
        direction = residual + (norm_next / norm_now) * direction
        norm_now = norm_next
    return solution, residual
```

```python
import jax
import jax.numpy as jnp
from jax import lax
from jax.experimental import pallas as pl
from jax.experimental.pallas import tpu as pltpu
from jax.sharding import PartitionSpec as P

STEPS = 2
NX, NY, NZ = 4, 8, 12
ROWS = 16
RANK = 256
BLOCK = 256
NIB = 48
HALF = RANK // 2
WIDE = 4 * NZ * ROWS
CHUNKS = NX * NY * NZ * ROWS // WIDE
BLOCKS_A_CHUNK = WIDE // 128
PRIME = 65521
SQUARE = 32749 * 32749 % PRIME
ROW_STEP = (7883 * SQUARE + 31) % PRIME
COL_STEP = (6151 * SQUARE + 17) % PRIME
RIDGE = 0.5
MESH = pl.DeviceIdType.MESH


def wrap(value, size):
    return lax.rem(value + size, jnp.int32(size))


def below(value):
    return jnp.where(value >= PRIME, value - PRIME, value)


def kernel(
    items, users, tile_items, tile_seed, tile_count, sol_out, res_out,
    gathered, conf, lane_hash, lane_live, row_hash, gram, total, partial, arrived, vec, solv, resv,
    zs, zr, ys, yr, xs, xr, us, ur, vs, vr, ws, wr, es, er,
):
    blk = lax.axis_index("blk")
    core = lax.axis_index("grp")
    z = lax.rem(blk, NZ)
    line = lax.div(blk, NZ)
    y = lax.rem(line, NY)
    x = lax.div(line, NY)

    def dev(xx, yy, zz, cc=core):
        return ((xx * NY + yy) * NZ + zz, cc)

    def rc(src, dst, send, recv, to):
        return pltpu.make_async_remote_copy(
            src_ref=src, dst_ref=dst, send_sem=send, recv_sem=recv, device_id=to, device_id_type=MESH
        )

    sibling = dev(x, y, z, 1 - core)
    barrier = pltpu.get_barrier_semaphore()

    def greet(to):
        pl.semaphore_signal(barrier, inc=1, device_id=to, device_id_type=MESH)

    def z_line(d, back):
        zz = wrap(z - d, NZ) if back else z
        return rc(items, gathered.at[x, y, zz], zs.at[d - 1], zr.at[d - 1], dev(x, y, wrap(z + d - NZ, NZ)))

    def y_ring(s, sign, back):
        far = s + 1 if back else s
        yy = wrap(y - far, NY) if sign == 0 else wrap(y + far - NY, NY)
        to = dev(x, wrap(y + 1 - NY, NY) if sign == 0 else wrap(y - 1, NY), z)
        ref = gathered.at[x, yy] if s < 3 else gathered.at[x, yy, pl.ds(6 * sign, 6)]
        return rc(ref, ref, ys.at[sign * 4 + s], yr.at[sign * 4 + s], to)

    def x_ring(e, yy, kind, back):
        sign = kind % 2
        far = kind // 2 + (1 if back else 0)
        xx = wrap(x - far, NX) if sign == 0 else wrap(x + far - NX, NX)
        to = dev(wrap(x + 1 - NX, NX) if sign == 0 else wrap(x - 1, NX), y, z)
        ref = gathered.at[xx, yy] if kind < 2 else gathered.at[xx, yy, pl.ds(6 * sign, 6)]
        return rc(ref, ref, xs.at[e * 4 + kind], xr.at[e * 4 + kind], to)

    offsets = (0, -1, 1, -2, 2, -3, 3, 4)

    def y_of(e):
        return wrap(y + offsets[e] - (NY if offsets[e] > 0 else 0), NY)

    def x_send(e):
        for kind in (0, 1):
            x_ring(e, y_of(e), kind, False).start()

    def x_forward(e):
        for kind in (0, 1):
            x_ring(e, y_of(e), kind, True).wait_recv()
            x_ring(e, y_of(e), kind + 2, False).start()

    def x_line(d, back):
        xx = wrap(x - d, NX) if back else x
        return rc(items, gathered.at[xx, y, z], us.at[d - 1], ur.at[d - 1], dev(wrap(x + d - NX, NX), y, z))

    def y_line(d, back):
        yy = wrap(y - d, NY) if back else y
        ref = gathered.at[:, yy, z]
        return rc(ref, ref, vs.at[d - 1], vr.at[d - 1], dev(x, wrap(y + d - NY, NY), z))

    def z_ring(s, k, sign, back):
        far = s + 1 if back else s
        zz = wrap(z - far, NZ) if sign == 0 else wrap(z + far - NZ, NZ)
        to = dev(x, y, wrap(z + 1 - NZ, NZ) if sign == 0 else wrap(z - 1, NZ))
        ref = gathered.at[pl.ds(2 * k, 2), :, zz]
        sem = (s * 2 + k) * 2 + sign
        return rc(ref, ref, ws.at[sem], wr.at[sem], to)

    ring_parts = [[(k, sign) for k in range(2) for sign in range(2)] for _ in range(5)] + [[(0, 0), (1, 1)]]

    gathered[x, y, z] = items[...]

    @pl.when(core == 0)
    def _():
        for d in range(1, NZ):
            greet(dev(x, y, wrap(z + d - NZ, NZ)))
        greet(dev(x, wrap(y + 1 - NY, NY), z))
        greet(dev(x, wrap(y - 1, NY), z))
        greet(dev(wrap(x + 1 - NX, NX), y, z))
        greet(dev(wrap(x - 1, NX), y, z))
        greet(sibling)
        pl.semaphore_wait(barrier, NZ - 1 + 5)
        for d in range(1, NZ):
            z_line(d, False).start()

    @pl.when(core == 1)
    def _():
        for d in range(1, NX):
            greet(dev(wrap(x + d - NX, NX), y, z))
        for d in range(1, NY):
            greet(dev(x, wrap(y + d - NY, NY), z))
        greet(dev(x, y, wrap(z + 1 - NZ, NZ)))
        greet(dev(x, y, wrap(z - 1, NZ)))
        greet(sibling)
        pl.semaphore_wait(barrier, NX - 1 + NY - 1 + 3)
        for d in range(1, NX):
            x_line(d, False).start()

    slot = lax.broadcasted_iota(jnp.int32, (NIB, NIB), 1)
    wanted = lax.broadcasted_iota(jnp.int32, (NIB, NIB), 0)
    seed = lax.rem(lax.rem(lax.rem(tile_seed[...] * 509, PRIME) * 32749, PRIME) * 32749, PRIME)
    match = jnp.where((tile_items[...] == wanted) & (slot < tile_count[0]), 1.0, 0.0)
    live = jnp.sum(match, axis=1, keepdims=True)
    seed_of = jnp.sum(match * seed.astype(jnp.float32), axis=1, keepdims=True).astype(jnp.int32)
    lane = lax.broadcasted_iota(jnp.int32, (NIB, 128), 1)
    column = lax.div(lane, ROWS) * (2 * ROWS) + core * ROWS + lax.rem(lane, ROWS)
    lane_hash[...] = below(lax.rem(column * COL_STEP, PRIME) + seed_of)
    lane_live[...] = jnp.broadcast_to(live, (NIB, 128))
    row_hash[...] = lax.rem(lax.broadcasted_iota(jnp.int32, (BLOCK, 128), 0) * ROW_STEP, PRIME)

    def fill(chunk):
        for piece in range(BLOCKS_A_CHUNK):
            i = chunk * BLOCKS_A_CHUNK + piece
            hashed = below(row_hash[...] + lane_hash[pl.ds(i, 1), :])
            alive = lane_live[pl.ds(i, 1), :]
            value = lax.shift_right_logical(hashed, 1).astype(jnp.float32)
            value = value - 1000.0 * jnp.floor(value * 0.001 + 0.0005)
            weight = 0.5 * alive + (0.0035 * alive) * value
            conf[chunk, :, piece * 128:(piece + 1) * 128] = jnp.where((hashed & 1) == 1, weight, 0.0)

    pl.loop(0, CHUNKS)(fill)

    @pl.when(core == 0)
    def _():
        for d in range(1, NZ):
            z_line(d, True).wait_recv()
        y_ring(0, 0, False).start()
        y_ring(0, 1, False).start()
        x_send(0)
        for s in range(3):
            for sign in (0, 1):
                y_ring(s, sign, True).wait_recv()
                y_ring(s + 1, sign, False).start()
                x_send(2 * s + 1 + sign)
            for e in ((0,), (1, 2), (3, 4))[s]:
                x_forward(e)
        y_ring(3, 0, True).wait_recv()
        y_ring(3, 1, True).wait_recv()
        x_send(7)
        for e in (5, 6, 7):
            x_forward(e)
        for e in range(NY):
            for kind in (2, 3):
                x_ring(e, y_of(e), kind, True).wait_recv()
        for d in range(1, NZ):
            z_line(d, False).wait_send()
        for s in range(4):
            for sign in (0, 1):
                y_ring(s, sign, False).wait_send()
        for e in range(NY):
            for kind in range(4):
                x_ring(e, y_of(e), kind, False).wait_send()

    @pl.when(core == 1)
    def _():
        for d in range(1, NX):
            x_line(d, True).wait_recv()
        for d in range(1, NY):
            y_line(d, False).start()
        for d in range(1, NY):
            y_line(d, True).wait_recv()
        for s in range(6):
            for k, sign in ring_parts[s]:
                if s:
                    z_ring(s - 1, k, sign, True).wait_recv()
                z_ring(s, k, sign, False).start()
        for k, sign in ((0, 1), (1, 0)):
            z_ring(4, k, sign, True).wait_recv()
        for k, sign in ring_parts[5]:
            z_ring(5, k, sign, True).wait_recv()
        for d in range(1, NX):
            x_line(d, False).wait_send()
        for d in range(1, NY):
            y_line(d, False).wait_send()
        for s in range(6):
            for k, sign in ring_parts[s]:
                z_ring(s, k, sign, False).wait_send()

    def item_chunk(chunk):
        rows = gathered[lax.div(chunk, 2), pl.ds(lax.rem(chunk, 2) * 4, 4)]
        return rows.reshape(WIDE, RANK)

    def sweep(first):
        user_rows = vec[...].astype(jnp.bfloat16)

        def add(chunk):
            rows = item_chunk(chunk)
            scores = lax.dot_general(user_rows, rows, (((1,), (1,)), ((), ())), preferred_element_type=jnp.float32)
            trust = conf[chunk]
            weighted = (trust * scores).astype(jnp.bfloat16)
            term = jnp.dot(weighted, rows, preferred_element_type=jnp.float32)
            if first:
                target = jnp.where(trust > 0.0, trust + 1.0, 0.0).astype(jnp.bfloat16)
                total[...] += jnp.dot(target, rows, preferred_element_type=jnp.float32) - term
                gram[...] += lax.dot_general(
                    rows, rows, (((0,), (0,)), ((), ())), preferred_element_type=jnp.float32
                )
            else:
                total[...] += term

        total[...] = jnp.zeros_like(total)
        if first:
            gram[...] = jnp.zeros_like(gram)
        pl.loop(0, CHUNKS)(add)

    def whole(value):
        return jnp.dot(value, gram[...], precision=lax.Precision.HIGHEST, preferred_element_type=jnp.float32)

    def exchange(number, mine):
        partial[number] = mine
        copy = rc(partial.at[number], arrived.at[number], es.at[number], er.at[number], sibling)
        copy.start()
        copy.wait()
        return partial[number] + arrived[number]

    vec[...] = users[...]
    sweep(True)
    start = users[...]
    residual = exchange(0, total[...] - whole(start)) - RIDGE * start
    solv[...] = start
    resv[...] = residual
    vec[...] = residual
    norm = jnp.sum(residual * residual, axis=1, keepdims=True)
    for number in range(STEPS):
        sweep(False)
        applied = exchange(number + 1, whole(vec[...]) + total[...]) + RIDGE * vec[...]
        direction = vec[...]
        step = norm / jnp.sum(direction * applied, axis=1, keepdims=True)
        solv[...] = solv[...] + step * direction
        residual = resv[...] - step * applied
        resv[...] = residual
        following = jnp.sum(residual * residual, axis=1, keepdims=True)
        if number + 1 < STEPS:
            vec[...] = residual + (following / norm) * direction
        norm = following

    for side in (0, 1):
        @pl.when(core == side)
        def _():
            sol_out[...] = solv[:, side * HALF:(side + 1) * HALF]
            res_out[...] = resv[:, side * HALF:(side + 1) * HALF]


def on_device(item_factors, user_start, tile_items, tile_count, tile_seed):
    vmem = pl.BlockSpec(memory_space=pltpu.VMEM)
    whole = (BLOCK, RANK)
    dma = pltpu.SemaphoreType.DMA
    return pl.pallas_call(
        kernel,
        out_shape=[jax.ShapeDtypeStruct((BLOCK, HALF), jnp.float32)] * 2,
        in_specs=[vmem, vmem, vmem, vmem, pl.BlockSpec(memory_space=pltpu.SMEM)],
        out_specs=[vmem, vmem],
        scratch_shapes=[
            pltpu.VMEM((NX, NY, NZ, ROWS, RANK), jnp.bfloat16),
            pltpu.VMEM((CHUNKS, BLOCK, WIDE), jnp.float32),
            pltpu.VMEM((NIB, 128), jnp.int32),
            pltpu.VMEM((NIB, 128), jnp.float32),
            pltpu.VMEM((BLOCK, 128), jnp.int32),
            pltpu.VMEM((RANK, RANK), jnp.float32),
            pltpu.VMEM(whole, jnp.float32),
            pltpu.VMEM((STEPS + 1,) + whole, jnp.float32),
            pltpu.VMEM((STEPS + 1,) + whole, jnp.float32),
            pltpu.VMEM(whole, jnp.float32),
            pltpu.VMEM(whole, jnp.float32),
            pltpu.VMEM(whole, jnp.float32),
            dma((NZ - 1,)), dma((NZ - 1,)),
            dma((8,)), dma((8,)),
            dma((32,)), dma((32,)),
            dma((NX - 1,)), dma((NX - 1,)),
            dma((NY - 1,)), dma((NY - 1,)),
            dma((24,)), dma((24,)),
            dma((STEPS + 1,)), dma((STEPS + 1,)),
        ],
        compiler_params=pltpu.CompilerParams(
            collective_id=0, has_side_effects=True, vmem_limit_bytes=40 * 1024 * 1024
        ),
    )(item_factors, user_start, tile_items, tile_seed, tile_count)


def solution(mesh):
    return jax.shard_map(
        on_device,
        mesh=mesh,
        in_specs=(
            P(("blk", "grp"), None),
            P("blk", None),
            P("blk", None),
            P("blk"),
            P("blk", None),
        ),
        out_specs=(P("blk", "grp"), P("blk", "grp")),
        check_vma=False,
    )
```

```python
import jax
import jax.numpy as jnp
from jax import lax
from jax.experimental import pallas as pl
from jax.experimental.pallas import tpu as pltpu
from jax.sharding import PartitionSpec as P

STEPS = 2
NX, NY, NZ = 4, 8, 12
CHIPS = NX * NY * NZ
ROWS = 16
RANK = 256
BLOCK = 256
NIB = 48
HALF = RANK // 2
GROUPS = CHIPS * ROWS // 128
UNIT = 256
CHUNKS = 8
CHIPS_A_CHUNK = CHIPS // CHUNKS
GROUPS_A_CHUNK = GROUPS // CHUNKS
PRIME = 65521
SQUARE = 32749 * 32749 % PRIME
ROW_STEP = (7883 * SQUARE + 31) % PRIME
COL_STEP = (6151 * SQUARE + 17) % PRIME
RIDGE = 0.5
MESH = pl.DeviceIdType.MESH


def below(value):
    return jnp.where(value >= PRIME, value - PRIME, value)


def matmul(a, b, dims=((1,), (0,))):
    return lax.dot_general(a, b, (dims, ((), ())), preferred_element_type=jnp.float32)


def kernel(
    items, users, tile_items, tile_seed, tile_count, sol_out, res_out,
    gathered, conf, slots, row_hash, gram, total, partial, arrived, vec, vec16, solv, resv,
    s1, r1, s2, r2, s3, r3, es, er, local,
):
    blk = lax.axis_index("blk")
    core = lax.axis_index("grp")
    z = lax.rem(blk, NZ)
    line = lax.div(blk, NZ)
    y = lax.rem(line, NY)
    x = lax.div(line, NY)

    def dev(xx, yy, zz, cc=core):
        return ((xx * NY + yy) * NZ + zz, cc)

    def rc(src, dst, send, recv, to):
        return pltpu.make_async_remote_copy(
            src_ref=src, dst_ref=dst, send_sem=send, recv_sem=recv, device_id=to, device_id_type=MESH
        )

    def around(value, size):
        ahead = [value] + [jnp.where(value + d >= size, value + d - size, value + d) for d in range(1, size)]
        return lambda d: ahead[d % size]

    x_at, y_at, z_at = around(x, NX), around(y, NY), around(z, NZ)

    def by(xd, yd, zd):
        return dev(x_at(xd), y_at(yd), z_at(zd))

    sibling = dev(x, y, z, 1 - core)
    barrier = pltpu.get_barrier_semaphore()

    def greet(to):
        pl.semaphore_signal(barrier, inc=1, device_id=to, device_id_type=MESH)

    def chip0(xx, yy, zz):
        return (yy * NX + xx) * NZ + zz

    def z_line(d, back):
        ref = gathered.at[chip0(x, y, z_at(-d) if back else z)]
        return rc(items, ref, s1.at[d - 1], r1.at[d - 1], by(0, 0, d))

    x_far = (0, 1, -1, 2)

    def x_line(e, back):
        ref = gathered.at[pl.ds(chip0(x_at(-x_far[e]) if back else x, y, 0), NZ)]
        return rc(ref, ref, s2.at[e], r2.at[e], by(x_far[e], 0, 0))

    def y_ring(s, e, side, back):
        sign = 1 - 2 * side
        ref = gathered.at[pl.ds(chip0(x_at(-x_far[e]), y_at(-sign * (s + (1 if back else 0))), 0), NZ)]
        sem = (s * 4 + e) * 2 + side
        return rc(ref, ref, s3.at[sem], r3.at[sem], by(0, sign, 0))

    def chip1(xx, yy, zz):
        return (zz * NX + xx) * NY + yy

    plane = [(xd, yd) for xd in range(NX) for yd in range(NY)][1:]
    plane = sorted(plane, key=lambda m: -min(m[0], NX - m[0]) - min(m[1], NY - m[1]))

    def plane_send(i, back):
        xd, yd = plane[i]
        ref = gathered.at[chip1(x_at(-xd), y_at(-yd), z) if back else chip1(x, y, z)]
        return rc(items, ref, s1.at[i], r1.at[i], by(xd, yd, 0))

    def z_ring(s, e, side, back):
        sign = 1 - 2 * side
        ref = gathered.at[pl.ds(chip1(e, 0, z_at(-sign * (s + (1 if back else 0)))), NY)]
        sem = (s * 4 + e) * 2 + side
        return rc(ref, ref, s3.at[sem], r3.at[sem], by(0, 0, sign))

    def moves(last):
        return [[(e, side) for e in range(NX) for side in (0, 1) if s < last or e % 2 == side] for s in range(last + 1)]

    y_moves, z_moves = moves(NY // 2 - 1), moves(NZ // 2 - 1)

    def fetch(number, src, dst):
        return pltpu.make_async_copy(src, dst, local.at[number])

    own = jnp.where(core == 0, chip0(x, y, z), chip1(x, y, z))
    fetched = [
        fetch(0, items, gathered.at[own]), fetch(1, users, vec),
        fetch(2, tile_items, slots.at[pl.ds(0, 1)]), fetch(3, tile_seed, slots.at[pl.ds(8, 1)]),
    ]
    for copy in fetched:
        copy.start()

    @pl.when(core == 0)
    def _():
        for far in [(0, 0, d) for d in range(1, NZ)] + [(d, 0, 0) for d in range(1, NX)] + [(0, 1, 0), (0, -1, 0)]:
            greet(by(*far))
        greet(sibling)
        pl.semaphore_wait(barrier, NZ - 1 + NX - 1 + 3)
        for d in (6, 5, 7, 4, 8, 3, 9, 2, 10, 1, 11):
            z_line(d, False).start()

    @pl.when(core == 1)
    def _():
        for far in [(xd, yd, 0) for xd, yd in plane] + [(0, 0, 1), (0, 0, -1)]:
            greet(by(*far))
        greet(sibling)
        pl.semaphore_wait(barrier, len(plane) + 3)
        for i in range(len(plane)):
            plane_send(i, False).start()

    for copy in fetched:
        copy.wait()
    start = vec[...]
    vec16[...] = start.astype(jnp.bfloat16)
    total[...] = jnp.zeros_like(total)
    gram[...] = jnp.zeros_like(gram)

    slot = lax.broadcasted_iota(jnp.int32, (NIB, NIB), 1)
    wanted = lax.broadcasted_iota(jnp.int32, (NIB, NIB), 0)
    seeds = slots[8:9, 0:NIB]
    seeds = lax.rem(lax.rem(lax.rem(seeds * 509, PRIME) * 32749, PRIME) * 32749, PRIME)

    def upright(row):
        return jnp.sum(jnp.where(slot == wanted, row.astype(jnp.float32), 0.0), axis=1, keepdims=True)

    seed_col = jnp.broadcast_to(upright(seeds), (NIB, 128))
    item_col = upright(slots[0:1, 0:NIB])
    live_slot = lax.broadcasted_iota(jnp.int32, (NIB, 1), 0) < tile_count[0]
    item_col = jnp.broadcast_to(jnp.where(live_slot, item_col, -1.0), (NIB, 128))
    lane = lax.broadcasted_iota(jnp.int32, (1, 128), 1)
    row_hash[...] = lax.rem(lax.broadcasted_iota(jnp.int32, (BLOCK, 128), 0) * ROW_STEP, PRIME)

    def lanes(group):
        place = group * 8 + lax.div(lane, ROWS)
        yy0, rest0 = lax.div(place, NX * NZ), lax.rem(place, NX * NZ)
        zz1, rest1 = lax.div(place, NX * NY), lax.rem(place, NX * NY)
        chip = jnp.where(
            core == 0,
            (lax.div(rest0, NZ) * NY + yy0) * NZ + lax.rem(rest0, NZ),
            rest1 * NZ + zz1,
        )
        match = jnp.where(item_col == lax.div(chip, 8).astype(jnp.float32), 1.0, 0.0)
        live = jnp.sum(match, axis=0, keepdims=True)
        seed = jnp.sum(match * seed_col, axis=0, keepdims=True).astype(jnp.int32)
        column = lax.rem(chip, 8) * (2 * ROWS) + core * ROWS + lax.rem(lane, ROWS)
        return below(lax.rem(column * COL_STEP, PRIME) + seed), live

    def fill(group):
        offset, alive = lanes(group)
        hashed = below(row_hash[...] + offset)
        value = lax.shift_right_logical(hashed, 1).astype(jnp.float32)
        value = value - 1000.0 * jnp.floor(value * 0.001 + 0.0005)
        weight = 0.5 * alive + (0.0035 * alive) * value
        conf[group] = jnp.where((hashed & 1) == 1, weight, 0.0)

    pl.loop(0, GROUPS)(fill)

    def unit(place):
        rows = gathered[pl.ds(place * (UNIT // ROWS), UNIT // ROWS)].reshape(UNIT, RANK)
        trust = jnp.concatenate([conf[place * 2 + half] for half in range(2)], axis=1)
        scores = matmul(vec16[...], rows, ((1,), (1,)))
        target = jnp.where(trust > 0.0, trust + 1.0, 0.0).astype(jnp.bfloat16)
        wanted_sum = matmul(target, rows)
        gram[...] += matmul(rows, rows, ((0,), (0,)))
        weighted = (trust * scores).astype(jnp.bfloat16)
        total[...] += wanted_sum - matmul(weighted, rows)

    def gather_ring(ring, steps, ready, units_of):
        pending = [(0, part) for part in range(units_of)]

        def some(count):
            for _ in range(min(count, len(pending))):
                far, part = pending.pop(0)
                unit(ready(far) * units_of + part)

        for s in range(len(steps)):
            for e, side in steps[s]:
                if s:
                    ring(s - 1, e, side, True).wait_recv()
                    ring(s, e, side, False).start()
                    if (e, side) != steps[s][0]:
                        some(1)
            if s and s < len(steps) - 1:
                pending.extend((far, part) for far in (-s, s) for part in range(units_of))
        last = len(steps) - 1
        for e, side in steps[last - 1]:
            if (e, side) not in steps[last]:
                ring(last - 1, e, side, True).wait_recv()
        pending.extend((far, part) for far in (-last, last) for part in range(units_of))
        some(2 * units_of)
        for e, side in steps[last]:
            ring(last, e, side, True).wait_recv()
        pending.extend((last + 1, part) for part in range(units_of))
        some(len(pending))

    @pl.when(core == 0)
    def _():
        for d in range(1, NZ):
            z_line(d, True).wait_recv()
        for e in range(1, NX):
            x_line(e, False).start()
        for e in range(NX):
            if e:
                x_line(e, True).wait_recv()
            y_ring(0, e, 0, False).start()
            y_ring(0, e, 1, False).start()
        gather_ring(y_ring, y_moves, y_at, 3)
        for d in range(1, NZ):
            z_line(d, False).wait_send()
        for e in range(1, NX):
            x_line(e, False).wait_send()
        for s in range(len(y_moves)):
            for e, side in y_moves[s]:
                y_ring(s, e, side, False).wait_send()

    @pl.when(core == 1)
    def _():
        for i in range(len(plane)):
            plane_send(i, True).wait_recv()
        for e, side in z_moves[0]:
            z_ring(0, e, side, False).start()
        gather_ring(z_ring, z_moves, z_at, 2)
        for i in range(len(plane)):
            plane_send(i, False).wait_send()
        for s in range(len(z_moves)):
            for e, side in z_moves[s]:
                z_ring(s, e, side, False).wait_send()

    def item_chunk(chunk):
        rows = gathered[pl.ds(chunk * CHIPS_A_CHUNK, CHIPS_A_CHUNK)]
        return rows.reshape(CHIPS_A_CHUNK * ROWS, RANK)

    def sweep():
        user_rows = vec16[...]
        acc = jnp.zeros((BLOCK, RANK), jnp.float32)
        scores = matmul(user_rows, item_chunk(0), ((1,), (1,)))
        for chunk in range(CHUNKS):
            later = matmul(user_rows, item_chunk(chunk + 1), ((1,), (1,))) if chunk + 1 < CHUNKS else None
            trust = jnp.concatenate([conf[chunk * GROUPS_A_CHUNK + k] for k in range(GROUPS_A_CHUNK)], axis=1)
            weighted = (trust * scores).astype(jnp.bfloat16)
            acc = acc + matmul(weighted, item_chunk(chunk))
            scores = later
        return acc

    def whole(value):
        return jnp.dot(value, gram[...], precision=lax.Precision.HIGHEST, preferred_element_type=jnp.float32)

    def exchange(number, mine):
        partial[number] = mine
        copy = rc(partial.at[number], arrived.at[number], es.at[number], er.at[number], sibling)
        copy.start()
        copy.wait()
        return partial[number] + arrived[number]

    start = vec[...]
    residual = exchange(0, total[...] - whole(start)) - RIDGE * start
    solv[...] = start
    resv[...] = residual
    vec[...] = residual
    vec16[...] = residual.astype(jnp.bfloat16)
    norm = jnp.sum(residual * residual, axis=1, keepdims=True)
    for number in range(STEPS):
        applied = exchange(number + 1, sweep() + whole(vec[...])) + RIDGE * vec[...]
        direction = vec[...]
        step = norm / jnp.sum(direction * applied, axis=1, keepdims=True)
        solv[...] = solv[...] + step * direction
        residual = resv[...] - step * applied
        resv[...] = residual
        following = jnp.sum(residual * residual, axis=1, keepdims=True)
        if number + 1 < STEPS:
            direction = residual + (following / norm) * direction
            vec[...] = direction
            vec16[...] = direction.astype(jnp.bfloat16)
        norm = following

    for side in (0, 1):
        @pl.when(core == side)
        def _():
            sol_out[...] = solv[:, side * HALF:(side + 1) * HALF]
            res_out[...] = resv[:, side * HALF:(side + 1) * HALF]


def on_device(item_factors, user_start, tile_items, tile_count, tile_seed):
    vmem = pl.BlockSpec(memory_space=pltpu.VMEM)
    hbm = pl.BlockSpec(memory_space=pltpu.HBM)
    whole = (BLOCK, RANK)
    dma = pltpu.SemaphoreType.DMA
    return pl.pallas_call(
        kernel,
        out_shape=[jax.ShapeDtypeStruct((BLOCK, HALF), jnp.float32)] * 2,
        in_specs=[hbm, hbm, hbm, hbm, pl.BlockSpec(memory_space=pltpu.SMEM)],
        out_specs=[vmem, vmem],
        scratch_shapes=[
            pltpu.VMEM((CHIPS, ROWS, RANK), jnp.bfloat16),
            pltpu.VMEM((GROUPS, BLOCK, 128), jnp.float32),
            pltpu.VMEM((16, NIB), jnp.int32),
            pltpu.VMEM((BLOCK, 128), jnp.int32),
            pltpu.VMEM((RANK, RANK), jnp.float32),
            pltpu.VMEM(whole, jnp.float32),
            pltpu.VMEM((STEPS + 1,) + whole, jnp.float32),
            pltpu.VMEM((STEPS + 1,) + whole, jnp.float32),
            pltpu.VMEM(whole, jnp.float32),
            pltpu.VMEM(whole, jnp.bfloat16),
            pltpu.VMEM(whole, jnp.float32),
            pltpu.VMEM(whole, jnp.float32),
            dma((31,)), dma((31,)),
            dma((NX,)), dma((NX,)),
            dma((48,)), dma((48,)),
            dma((STEPS + 1,)), dma((STEPS + 1,)),
            dma((4,)),
        ],
        compiler_params=pltpu.CompilerParams(
            collective_id=0, has_side_effects=True, vmem_limit_bytes=40 * 1024 * 1024
        ),
    )(item_factors, user_start, tile_items, tile_seed, tile_count)


def solution(mesh):
    return jax.shard_map(
        on_device,
        mesh=mesh,
        in_specs=(
            P(("blk", "grp"), None),
            P("blk", None),
            P("blk", None),
            P("blk"),
            P("blk", None),
        ),
        out_specs=(P("blk", "grp"), P("blk", "grp")),
        check_vma=False,
    )
```

```python
import jax
import jax.numpy as jnp
from jax import lax
from jax.experimental import pallas as pl
from jax.experimental.pallas import tpu as pltpu
from jax.sharding import PartitionSpec as P

STEPS = 2
NX, NY, NZ = 4, 8, 12
CHIPS = NX * NY * NZ
ROWS = 16
RANK = 256
BLOCK = 256
NIB = 48
HALF = RANK // 2
GROUPS = CHIPS * ROWS // 128
UNIT = 256
CHUNKS = 8
CHIPS_A_CHUNK = CHIPS // CHUNKS
GROUPS_A_CHUNK = GROUPS // CHUNKS
PRIME = 65521
SQUARE = 32749 * 32749 % PRIME
ROW_STEP = (7883 * SQUARE + 31) % PRIME
COL_STEP = (6151 * SQUARE + 17) % PRIME
RIDGE = 0.5
MESH = pl.DeviceIdType.MESH


def below(value):
    return jnp.where(value >= PRIME, value - PRIME, value)


def matmul(a, b, dims=((1,), (0,))):
    return lax.dot_general(a, b, (dims, ((), ())), preferred_element_type=jnp.float32)


def kernel(
    items, users, tile_items, tile_seed, tile_count, sol_out, res_out,
    gathered, conf, slots, row_hash, gram, gram_other, gram_sum, total, partial, arrived, vec, vec16, solv, resv,
    s1, r1, s2, r2, s3, r3, es, er, local,
):
    blk = lax.axis_index("blk")
    core = lax.axis_index("grp")
    z = lax.rem(blk, NZ)
    line = lax.div(blk, NZ)
    y = lax.rem(line, NY)
    x = lax.div(line, NY)

    def dev(xx, yy, zz, cc=core):
        return ((xx * NY + yy) * NZ + zz, cc)

    def rc(src, dst, send, recv, to):
        return pltpu.make_async_remote_copy(
            src_ref=src, dst_ref=dst, send_sem=send, recv_sem=recv, device_id=to, device_id_type=MESH
        )

    def around(value, size):
        ahead = [value] + [jnp.where(value + d >= size, value + d - size, value + d) for d in range(1, size)]
        return lambda d: ahead[d % size]

    x_at, y_at, z_at = around(x, NX), around(y, NY), around(z, NZ)

    def by(xd, yd, zd):
        return dev(x_at(xd), y_at(yd), z_at(zd))

    sibling = dev(x, y, z, 1 - core)
    barrier = pltpu.get_barrier_semaphore()

    def greet(to):
        pl.semaphore_signal(barrier, inc=1, device_id=to, device_id_type=MESH)

    def chip0(xx, yy, zz):
        return (yy * NX + xx) * NZ + zz

    def z_line(d, back):
        ref = gathered.at[chip0(x, y, z_at(-d) if back else z)]
        return rc(items, ref, s1.at[d - 1], r1.at[d - 1], by(0, 0, d))

    x_far = (0, 1, -1, 2)

    def x_line(e, back):
        ref = gathered.at[pl.ds(chip0(x_at(-x_far[e]) if back else x, y, 0), NZ)]
        return rc(ref, ref, s2.at[e], r2.at[e], by(x_far[e], 0, 0))

    def y_ring(s, e, side, back):
        sign = 1 - 2 * side
        place = chip0(x_at(-x_far[e // 2]), y_at(-sign * (s + (1 if back else 0))), e % 2 * 6)
        ref = gathered.at[pl.ds(place, 6)]
        sem = (s * 8 + e) * 2 + side
        return rc(ref, ref, s3.at[sem], r3.at[sem], by(0, sign, 0))

    def chip1(xx, yy, zz):
        return (zz * NX + xx) * NY + yy

    plane = [(xd, yd) for xd in range(NX) for yd in range(NY)][1:]
    plane = sorted(plane, key=lambda m: -min(m[0], NX - m[0]) - min(m[1], NY - m[1]))

    def plane_send(i, back):
        xd, yd = plane[i]
        ref = gathered.at[chip1(x_at(-xd), y_at(-yd), z) if back else chip1(x, y, z)]
        return rc(items, ref, s1.at[i], r1.at[i], by(xd, yd, 0))

    def z_ring(s, e, side, back):
        sign = 1 - 2 * side
        ref = gathered.at[pl.ds(chip1(e, 0, z_at(-sign * (s + (1 if back else 0)))), NY)]
        sem = (s * 4 + e) * 2 + side
        return rc(ref, ref, s3.at[sem], r3.at[sem], by(0, 0, sign))

    def moves(last, subs):
        return [[(e, side) for e in range(subs) for side in (0, 1) if s < last or e % 2 == side] for s in range(last + 1)]

    y_moves, z_moves = moves(NY // 2 - 1, 2 * NX), moves(NZ // 2 - 1, NX)

    def fetch(number, src, dst):
        return pltpu.make_async_copy(src, dst, local.at[number])

    own = jnp.where(core == 0, chip0(x, y, z), chip1(x, y, z))
    fetched = [
        fetch(0, items, gathered.at[own]), fetch(1, users, vec),
        fetch(2, tile_items, slots.at[pl.ds(0, 1)]), fetch(3, tile_seed, slots.at[pl.ds(8, 1)]),
    ]
    for copy in fetched:
        copy.start()

    @pl.when(core == 0)
    def _():
        for far in [(0, 0, d) for d in range(1, NZ)] + [(d, 0, 0) for d in range(1, NX)] + [(0, 1, 0), (0, -1, 0)]:
            greet(by(*far))
        greet(sibling)
        pl.semaphore_wait(barrier, NZ - 1 + NX - 1 + 3)
        for d in (6, 5, 7, 4, 8, 3, 9, 2, 10, 1, 11):
            z_line(d, False).start()

    @pl.when(core == 1)
    def _():
        for far in [(xd, yd, 0) for xd, yd in plane] + [(0, 0, 1), (0, 0, -1)]:
            greet(by(*far))
        greet(sibling)
        pl.semaphore_wait(barrier, len(plane) + 3)
        for i in range(len(plane)):
            plane_send(i, False).start()

    for copy in fetched:
        copy.wait()
    start = vec[...]
    vec16[...] = start.astype(jnp.bfloat16)
    total[...] = jnp.zeros_like(total)
    gram[...] = jnp.zeros_like(gram)

    slot = lax.broadcasted_iota(jnp.int32, (NIB, NIB), 1)
    wanted = lax.broadcasted_iota(jnp.int32, (NIB, NIB), 0)
    seeds = slots[8:9, 0:NIB]
    seeds = lax.rem(lax.rem(lax.rem(seeds * 509, PRIME) * 32749, PRIME) * 32749, PRIME)

    def upright(row):
        return jnp.sum(jnp.where(slot == wanted, row.astype(jnp.float32), 0.0), axis=1, keepdims=True)

    seed_col = jnp.broadcast_to(upright(seeds), (NIB, 128))
    item_col = upright(slots[0:1, 0:NIB])
    live_slot = lax.broadcasted_iota(jnp.int32, (NIB, 1), 0) < tile_count[0]
    item_col = jnp.broadcast_to(jnp.where(live_slot, item_col, -1.0), (NIB, 128))
    lane = lax.broadcasted_iota(jnp.int32, (1, 128), 1)
    row_hash[...] = lax.rem(lax.broadcasted_iota(jnp.int32, (BLOCK, 128), 0) * ROW_STEP, PRIME)

    def lanes(group):
        place = group * 8 + lax.div(lane, ROWS)
        yy0, rest0 = lax.div(place, NX * NZ), lax.rem(place, NX * NZ)
        zz1, rest1 = lax.div(place, NX * NY), lax.rem(place, NX * NY)
        chip = jnp.where(
            core == 0,
            (lax.div(rest0, NZ) * NY + yy0) * NZ + lax.rem(rest0, NZ),
            rest1 * NZ + zz1,
        )
        match = jnp.where(item_col == lax.div(chip, 8).astype(jnp.float32), 1.0, 0.0)
        live = jnp.sum(match, axis=0, keepdims=True)
        seed = jnp.sum(match * seed_col, axis=0, keepdims=True).astype(jnp.int32)
        column = lax.rem(chip, 8) * (2 * ROWS) + core * ROWS + lax.rem(lane, ROWS)
        return below(lax.rem(column * COL_STEP, PRIME) + seed), live

    def fill(group):
        offset, alive = lanes(group)
        hashed = below(row_hash[...] + offset)
        value = lax.shift_right_logical(hashed, 1).astype(jnp.float32)
        value = value - 1000.0 * jnp.floor(value * 0.001 + 0.0005)
        weight = 0.5 * alive + (0.0035 * alive) * value
        conf[group] = jnp.where((hashed & 1) == 1, weight, 0.0)

    pl.loop(0, GROUPS)(fill)

    def unit(place):
        rows = gathered[pl.ds(place * (UNIT // ROWS), UNIT // ROWS)].reshape(UNIT, RANK)
        trust = jnp.concatenate([conf[place * 2 + half] for half in range(2)], axis=1)
        scores = matmul(vec16[...], rows, ((1,), (1,)))
        target = jnp.where(trust > 0.0, trust + 1.0, 0.0).astype(jnp.bfloat16)
        wanted_sum = matmul(target, rows)
        gram[...] += matmul(rows, rows, ((0,), (0,)))
        weighted = (trust * scores).astype(jnp.bfloat16)
        total[...] += wanted_sum - matmul(weighted, rows)

    def gather_ring(ring, steps, ready, units_of):
        pending = [(0, part) for part in range(units_of)]

        def some(count):
            for _ in range(min(count, len(pending))):
                far, part = pending.pop(0)
                unit(ready(far) * units_of + part)

        for s in range(len(steps)):
            for e, side in steps[s]:
                if s:
                    ring(s - 1, e, side, True).wait_recv()
                    ring(s, e, side, False).start()
                    if (e, side) != steps[s][0]:
                        some(1)
            if s and s < len(steps) - 1:
                pending.extend((far, part) for far in (-s, s) for part in range(units_of))
        last = len(steps) - 1
        for e, side in steps[last - 1]:
            if (e, side) not in steps[last]:
                ring(last - 1, e, side, True).wait_recv()
        pending.extend((far, part) for far in (-last, last) for part in range(units_of))
        some(2 * units_of)
        for e, side in steps[last]:
            ring(last, e, side, True).wait_recv()
        pending.extend((last + 1, part) for part in range(units_of))
        some(len(pending))

    @pl.when(core == 0)
    def _():
        for d in range(1, NZ):
            z_line(d, True).wait_recv()
        for e in range(1, NX):
            x_line(e, False).start()
        for e in range(NX):
            if e:
                x_line(e, True).wait_recv()
            for piece in range(2):
                y_ring(0, 2 * e + piece, 0, False).start()
                y_ring(0, 2 * e + piece, 1, False).start()
        gather_ring(y_ring, y_moves, y_at, 3)
        for d in range(1, NZ):
            z_line(d, False).wait_send()
        for e in range(1, NX):
            x_line(e, False).wait_send()
        for s in range(len(y_moves)):
            for e, side in y_moves[s]:
                y_ring(s, e, side, False).wait_send()

    @pl.when(core == 1)
    def _():
        for i in range(len(plane)):
            plane_send(i, True).wait_recv()
        for e, side in z_moves[0]:
            z_ring(0, e, side, False).start()
        gather_ring(z_ring, z_moves, z_at, 2)
        for i in range(len(plane)):
            plane_send(i, False).wait_send()
        for s in range(len(z_moves)):
            for e, side in z_moves[s]:
                z_ring(s, e, side, False).wait_send()

    def item_chunk(chunk):
        rows = gathered[pl.ds(chunk * CHIPS_A_CHUNK, CHIPS_A_CHUNK)]
        return rows.reshape(CHIPS_A_CHUNK * ROWS, RANK)

    def sweep():
        user_rows = vec16[...]
        acc = jnp.zeros((BLOCK, RANK), jnp.float32)
        scores = matmul(user_rows, item_chunk(0), ((1,), (1,)))
        for chunk in range(CHUNKS):
            later = matmul(user_rows, item_chunk(chunk + 1), ((1,), (1,))) if chunk + 1 < CHUNKS else None
            trust = jnp.concatenate([conf[chunk * GROUPS_A_CHUNK + k] for k in range(GROUPS_A_CHUNK)], axis=1)
            weighted = (trust * scores).astype(jnp.bfloat16)
            acc = acc + matmul(weighted, item_chunk(chunk))
            scores = later
        return acc

    def whole(value, matrix):
        return jnp.dot(value, matrix, precision=lax.Precision.HIGHEST, preferred_element_type=jnp.float32)

    copies = [
        rc(partial.at[number], arrived.at[number], es.at[number], er.at[number], sibling) for number in range(STEPS + 1)
    ]
    gram_copy = rc(gram, gram_other, es.at[STEPS + 1], er.at[STEPS + 1], sibling)

    start = vec[...]
    partial[0] = total[...] - whole(start, gram[...])
    copies[0].start()
    gram_copy.start()
    copies[0].wait_recv()
    residual = partial[0] + arrived[0] - RIDGE * start
    solv[...] = start
    resv[...] = residual
    vec[...] = residual
    vec16[...] = residual.astype(jnp.bfloat16)
    norm = jnp.sum(residual * residual, axis=1, keepdims=True)
    for number in range(STEPS):
        partial[number + 1] = sweep()
        copies[number + 1].start()
        if number == 0:
            gram_copy.wait_recv()
            gram_sum[...] = gram[...] + gram_other[...]
        direction = vec[...]
        applied = whole(direction, gram_sum[...]) + RIDGE * direction
        copies[number + 1].wait_recv()
        applied = applied + (partial[number + 1] + arrived[number + 1])
        step = norm / jnp.sum(direction * applied, axis=1, keepdims=True)
        solv[...] = solv[...] + step * direction
        residual = resv[...] - step * applied
        resv[...] = residual
        following = jnp.sum(residual * residual, axis=1, keepdims=True)
        if number + 1 < STEPS:
            direction = residual + (following / norm) * direction
            vec[...] = direction
            vec16[...] = direction.astype(jnp.bfloat16)
        norm = following

    for copy in copies + [gram_copy]:
        copy.wait_send()

    for side in (0, 1):
        @pl.when(core == side)
        def _():
            sol_out[...] = solv[:, side * HALF:(side + 1) * HALF]
            res_out[...] = resv[:, side * HALF:(side + 1) * HALF]


def on_device(item_factors, user_start, tile_items, tile_count, tile_seed):
    vmem = pl.BlockSpec(memory_space=pltpu.VMEM)
    hbm = pl.BlockSpec(memory_space=pltpu.HBM)
    whole = (BLOCK, RANK)
    dma = pltpu.SemaphoreType.DMA
    return pl.pallas_call(
        kernel,
        out_shape=[jax.ShapeDtypeStruct((BLOCK, HALF), jnp.float32)] * 2,
        in_specs=[hbm, hbm, hbm, hbm, pl.BlockSpec(memory_space=pltpu.SMEM)],
        out_specs=[vmem, vmem],
        scratch_shapes=[
            pltpu.VMEM((CHIPS, ROWS, RANK), jnp.bfloat16),
            pltpu.VMEM((GROUPS, BLOCK, 128), jnp.float32),
            pltpu.VMEM((16, NIB), jnp.int32),
            pltpu.VMEM((BLOCK, 128), jnp.int32),
            pltpu.VMEM((RANK, RANK), jnp.float32),
            pltpu.VMEM((RANK, RANK), jnp.float32),
            pltpu.VMEM((RANK, RANK), jnp.float32),
            pltpu.VMEM(whole, jnp.float32),
            pltpu.VMEM((STEPS + 1,) + whole, jnp.float32),
            pltpu.VMEM((STEPS + 1,) + whole, jnp.float32),
            pltpu.VMEM(whole, jnp.float32),
            pltpu.VMEM(whole, jnp.bfloat16),
            pltpu.VMEM(whole, jnp.float32),
            pltpu.VMEM(whole, jnp.float32),
            dma((31,)), dma((31,)),
            dma((NX,)), dma((NX,)),
            dma((64,)), dma((64,)),
            dma((STEPS + 2,)), dma((STEPS + 2,)),
            dma((4,)),
        ],
        compiler_params=pltpu.CompilerParams(
            collective_id=0, has_side_effects=True, vmem_limit_bytes=40 * 1024 * 1024
        ),
    )(item_factors, user_start, tile_items, tile_seed, tile_count)


def solution(mesh):
    return jax.shard_map(
        on_device,
        mesh=mesh,
        in_specs=(
            P(("blk", "grp"), None),
            P("blk", None),
            P("blk", None),
            P("blk"),
            P("blk", None),
        ),
        out_specs=(P("blk", "grp"), P("blk", "grp")),
        check_vma=False,
    )
```

```python
import jax
import jax.numpy as jnp
from jax import lax
from jax.experimental import pallas as pl
from jax.experimental.pallas import tpu as pltpu
from jax.sharding import PartitionSpec as P

STEPS = 2
NX, NY, NZ = 4, 8, 12
CHIPS = NX * NY * NZ
ROWS = 16
RANK = 256
BLOCK = 256
NIB = 48
HALF = RANK // 2
GROUPS = CHIPS * ROWS // 128
UNIT = 256
CHUNKS = 8
CHIPS_A_CHUNK = CHIPS // CHUNKS
GROUPS_A_CHUNK = GROUPS // CHUNKS
PRIME = 65521
SQUARE = 32749 * 32749 % PRIME
ROW_STEP = (7883 * SQUARE + 31) % PRIME
COL_STEP = (6151 * SQUARE + 17) % PRIME
RIDGE = 0.5
MESH = pl.DeviceIdType.MESH


def below(value):
    return jnp.where(value >= PRIME, value - PRIME, value)


def matmul(a, b, dims=((1,), (0,))):
    return lax.dot_general(a, b, (dims, ((), ())), preferred_element_type=jnp.float32)


def kernel(
    items, users, tile_items, tile_seed, tile_count, sol_out, res_out,
    gathered, conf, slots, row_hash, gram, total, partial, arrived, vec, vec16, solv, resv,
    s1, r1, s2, r2, s3, r3, es, er, local,
):
    blk = lax.axis_index("blk")
    core = lax.axis_index("grp")
    z = lax.rem(blk, NZ)
    line = lax.div(blk, NZ)
    y = lax.rem(line, NY)
    x = lax.div(line, NY)

    def dev(xx, yy, zz, cc=core):
        return ((xx * NY + yy) * NZ + zz, cc)

    def rc(src, dst, send, recv, to):
        return pltpu.make_async_remote_copy(
            src_ref=src, dst_ref=dst, send_sem=send, recv_sem=recv, device_id=to, device_id_type=MESH
        )

    def around(value, size):
        ahead = [value] + [jnp.where(value + d >= size, value + d - size, value + d) for d in range(1, size)]
        return lambda d: ahead[d % size]

    x_at, y_at, z_at = around(x, NX), around(y, NY), around(z, NZ)

    def by(xd, yd, zd):
        return dev(x_at(xd), y_at(yd), z_at(zd))

    sibling = dev(x, y, z, 1 - core)
    barrier = pltpu.get_barrier_semaphore()

    def greet(to):
        pl.semaphore_signal(barrier, inc=1, device_id=to, device_id_type=MESH)

    def chip0(xx, yy, zz):
        return (yy * NZ + zz) * NX + xx

    def x_line(d, back):
        ref = gathered.at[chip0(x_at(-d) if back else x, y, z)]
        return rc(items, ref, s1.at[d - 1], r1.at[d - 1], by(d, 0, 0))

    def z_line(d, back):
        ref = gathered.at[pl.ds(chip0(0, y, z_at(-d) if back else z), NX)]
        return rc(ref, ref, s2.at[d - 1], r2.at[d - 1], by(0, 0, d))

    def y_ring(s, e, side, back):
        sign = 1 - 2 * side
        ref = gathered.at[pl.ds(chip0(0, y_at(-sign * (s + (1 if back else 0))), 3 * e), 3 * NX)]
        sem = (s * 4 + e) * 2 + side
        return rc(ref, ref, s3.at[sem], r3.at[sem], by(0, sign, 0))

    def chip1(xx, yy, zz):
        return (zz * NX + xx) * NY + yy

    plane = [(xd, yd) for xd in range(NX) for yd in range(NY)][1:]
    plane = sorted(plane, key=lambda m: -min(m[0], NX - m[0]) - min(m[1], NY - m[1]))

    def plane_send(i, back):
        xd, yd = plane[i]
        ref = gathered.at[chip1(x_at(-xd), y_at(-yd), z) if back else chip1(x, y, z)]
        return rc(items, ref, s1.at[i], r1.at[i], by(xd, yd, 0))

    def z_ring(s, e, side, back):
        sign = 1 - 2 * side
        ref = gathered.at[pl.ds(chip1(e, 0, z_at(-sign * (s + (1 if back else 0)))), NY)]
        sem = (s * 4 + e) * 2 + side
        return rc(ref, ref, s3.at[sem], r3.at[sem], by(0, 0, sign))

    def moves(last):
        return [[(e, side) for e in range(NX) for side in (0, 1) if s < last or e % 2 == side] for s in range(last + 1)]

    y_moves, z_moves = moves(NY // 2 - 1), moves(NZ // 2 - 1)

    def fetch(number, src, dst):
        return pltpu.make_async_copy(src, dst, local.at[number])

    own = jnp.where(core == 0, chip0(x, y, z), chip1(x, y, z))
    fetched = [
        fetch(0, items, gathered.at[own]), fetch(1, users, vec),
        fetch(2, tile_items, slots.at[pl.ds(0, 1)]), fetch(3, tile_seed, slots.at[pl.ds(8, 1)]),
    ]
    for copy in fetched:
        copy.start()

    @pl.when(core == 0)
    def _():
        for far in [(0, 0, d) for d in range(1, NZ)] + [(d, 0, 0) for d in range(1, NX)] + [(0, 1, 0), (0, -1, 0)]:
            greet(by(*far))
        greet(sibling)
        pl.semaphore_wait(barrier, NZ - 1 + NX - 1 + 3)
        for d in (2, 1, 3):
            x_line(d, False).start()

    @pl.when(core == 1)
    def _():
        for far in [(xd, yd, 0) for xd, yd in plane] + [(0, 0, 1), (0, 0, -1)]:
            greet(by(*far))
        greet(sibling)
        pl.semaphore_wait(barrier, len(plane) + 3)
        for i in range(len(plane)):
            plane_send(i, False).start()

    for copy in fetched:
        copy.wait()
    start = vec[...]
    vec16[...] = start.astype(jnp.bfloat16)
    total[...] = jnp.zeros_like(total)
    gram[...] = jnp.zeros_like(gram)

    slot = lax.broadcasted_iota(jnp.int32, (NIB, NIB), 1)
    wanted = lax.broadcasted_iota(jnp.int32, (NIB, NIB), 0)
    seeds = slots[8:9, 0:NIB]
    seeds = lax.rem(lax.rem(lax.rem(seeds * 509, PRIME) * 32749, PRIME) * 32749, PRIME)

    def upright(row):
        return jnp.sum(jnp.where(slot == wanted, row.astype(jnp.float32), 0.0), axis=1, keepdims=True)

    seed_col = jnp.broadcast_to(upright(seeds), (NIB, 128))
    item_col = upright(slots[0:1, 0:NIB])
    live_slot = lax.broadcasted_iota(jnp.int32, (NIB, 1), 0) < tile_count[0]
    item_col = jnp.broadcast_to(jnp.where(live_slot, item_col, -1.0), (NIB, 128))
    lane = lax.broadcasted_iota(jnp.int32, (1, 128), 1)
    row_hash[...] = lax.rem(lax.broadcasted_iota(jnp.int32, (BLOCK, 128), 0) * ROW_STEP, PRIME)

    def lanes(group):
        place = group * 8 + lax.div(lane, ROWS)
        yy0, rest0 = lax.div(place, NX * NZ), lax.rem(place, NX * NZ)
        zz1, rest1 = lax.div(place, NX * NY), lax.rem(place, NX * NY)
        chip = jnp.where(
            core == 0,
            (lax.rem(rest0, NX) * NY + yy0) * NZ + lax.div(rest0, NX),
            rest1 * NZ + zz1,
        )
        match = jnp.where(item_col == lax.div(chip, 8).astype(jnp.float32), 1.0, 0.0)
        live = jnp.sum(match, axis=0, keepdims=True)
        seed = jnp.sum(match * seed_col, axis=0, keepdims=True).astype(jnp.int32)
        column = lax.rem(chip, 8) * (2 * ROWS) + core * ROWS + lax.rem(lane, ROWS)
        return below(lax.rem(column * COL_STEP, PRIME) + seed), live

    def fill(group):
        offset, alive = lanes(group)
        hashed = below(row_hash[...] + offset)
        value = lax.shift_right_logical(hashed, 1).astype(jnp.float32)
        value = value - 1000.0 * jnp.floor(value * 0.001 + 0.0005)
        weight = 0.5 * alive + (0.0035 * alive) * value
        conf[group] = jnp.where((hashed & 1) == 1, weight, 0.0)

    pl.loop(0, GROUPS)(fill)

    def unit(place):
        rows = gathered[pl.ds(place * (UNIT // ROWS), UNIT // ROWS)].reshape(UNIT, RANK)
        trust = jnp.concatenate([conf[place * 2 + half] for half in range(2)], axis=1)
        scores = matmul(vec16[...], rows, ((1,), (1,)))
        target = jnp.where(trust > 0.0, trust + 1.0, 0.0).astype(jnp.bfloat16)
        wanted_sum = matmul(target, rows)
        gram[...] += matmul(rows, rows, ((0,), (0,)))
        weighted = (trust * scores).astype(jnp.bfloat16)
        total[...] += wanted_sum - matmul(weighted, rows)

    def gather_ring(ring, steps, ready, units_of):
        pending = [(0, part) for part in range(units_of)]

        def some(count):
            for _ in range(min(count, len(pending))):
                far, part = pending.pop(0)
                unit(ready(far) * units_of + part)

        for s in range(len(steps)):
            for e, side in steps[s]:
                if s:
                    ring(s - 1, e, side, True).wait_recv()
                    ring(s, e, side, False).start()
                    if (e, side) != steps[s][0]:
                        some(1)
            if s and s < len(steps) - 1:
                pending.extend((far, part) for far in (-s, s) for part in range(units_of))
        last = len(steps) - 1
        for e, side in steps[last - 1]:
            if (e, side) not in steps[last]:
                ring(last - 1, e, side, True).wait_recv()
        pending.extend((far, part) for far in (-last, last) for part in range(units_of))
        some(2 * units_of)
        for e, side in steps[last]:
            ring(last, e, side, True).wait_recv()
        pending.extend((last + 1, part) for part in range(units_of))
        some(len(pending))

    @pl.when(core == 0)
    def _():
        for d in range(1, NX):
            x_line(d, True).wait_recv()
        for d in (6, 5, 7, 4, 8, 3, 9, 2, 10, 1, 11):
            z_line(d, False).start()
        for d in range(1, NZ):
            z_line(d, True).wait_recv()
        for e, side in y_moves[0]:
            y_ring(0, e, side, False).start()
        gather_ring(y_ring, y_moves, y_at, 3)
        for d in range(1, NZ):
            z_line(d, False).wait_send()
        for d in range(1, NX):
            x_line(d, False).wait_send()
        for s in range(len(y_moves)):
            for e, side in y_moves[s]:
                y_ring(s, e, side, False).wait_send()

    @pl.when(core == 1)
    def _():
        for i in range(len(plane)):
            plane_send(i, True).wait_recv()
        for e, side in z_moves[0]:
            z_ring(0, e, side, False).start()
        gather_ring(z_ring, z_moves, z_at, 2)
        for i in range(len(plane)):
            plane_send(i, False).wait_send()
        for s in range(len(z_moves)):
            for e, side in z_moves[s]:
                z_ring(s, e, side, False).wait_send()

    def item_chunk(chunk):
        rows = gathered[pl.ds(chunk * CHIPS_A_CHUNK, CHIPS_A_CHUNK)]
        return rows.reshape(CHIPS_A_CHUNK * ROWS, RANK)

    def sweep():
        user_rows = vec16[...]
        acc = jnp.zeros((BLOCK, RANK), jnp.float32)
        scores = matmul(user_rows, item_chunk(0), ((1,), (1,)))
        for chunk in range(CHUNKS):
            later = matmul(user_rows, item_chunk(chunk + 1), ((1,), (1,))) if chunk + 1 < CHUNKS else None
            trust = jnp.concatenate([conf[chunk * GROUPS_A_CHUNK + k] for k in range(GROUPS_A_CHUNK)], axis=1)
            weighted = (trust * scores).astype(jnp.bfloat16)
            acc = acc + matmul(weighted, item_chunk(chunk))
            scores = later
        return acc

    def whole(value):
        return jnp.dot(value, gram[...], precision=lax.Precision.HIGHEST, preferred_element_type=jnp.float32)

    def exchange(number, mine):
        partial[number] = mine
        copy = rc(partial.at[number], arrived.at[number], es.at[number], er.at[number], sibling)
        copy.start()
        copy.wait()
        return partial[number] + arrived[number]

    start = vec[...]
    residual = exchange(0, total[...] - whole(start)) - RIDGE * start
    solv[...] = start
    resv[...] = residual
    vec[...] = residual
    vec16[...] = residual.astype(jnp.bfloat16)
    norm = jnp.sum(residual * residual, axis=1, keepdims=True)
    for number in range(STEPS):
        applied = exchange(number + 1, sweep() + whole(vec[...])) + RIDGE * vec[...]
        direction = vec[...]
        step = norm / jnp.sum(direction * applied, axis=1, keepdims=True)
        solv[...] = solv[...] + step * direction
        residual = resv[...] - step * applied
        resv[...] = residual
        following = jnp.sum(residual * residual, axis=1, keepdims=True)
        if number + 1 < STEPS:
            direction = residual + (following / norm) * direction
            vec[...] = direction
            vec16[...] = direction.astype(jnp.bfloat16)
        norm = following

    for side in (0, 1):
        @pl.when(core == side)
        def _():
            sol_out[...] = solv[:, side * HALF:(side + 1) * HALF]
            res_out[...] = resv[:, side * HALF:(side + 1) * HALF]


def on_device(item_factors, user_start, tile_items, tile_count, tile_seed):
    vmem = pl.BlockSpec(memory_space=pltpu.VMEM)
    hbm = pl.BlockSpec(memory_space=pltpu.HBM)
    whole = (BLOCK, RANK)
    dma = pltpu.SemaphoreType.DMA
    return pl.pallas_call(
        kernel,
        out_shape=[jax.ShapeDtypeStruct((BLOCK, HALF), jnp.float32)] * 2,
        in_specs=[hbm, hbm, hbm, hbm, pl.BlockSpec(memory_space=pltpu.SMEM)],
        out_specs=[vmem, vmem],
        scratch_shapes=[
            pltpu.VMEM((CHIPS, ROWS, RANK), jnp.bfloat16),
            pltpu.VMEM((GROUPS, BLOCK, 128), jnp.float32),
            pltpu.VMEM((16, NIB), jnp.int32),
            pltpu.VMEM((BLOCK, 128), jnp.int32),
            pltpu.VMEM((RANK, RANK), jnp.float32),
            pltpu.VMEM(whole, jnp.float32),
            pltpu.VMEM((STEPS + 1,) + whole, jnp.float32),
            pltpu.VMEM((STEPS + 1,) + whole, jnp.float32),
            pltpu.VMEM(whole, jnp.float32),
            pltpu.VMEM(whole, jnp.bfloat16),
            pltpu.VMEM(whole, jnp.float32),
            pltpu.VMEM(whole, jnp.float32),
            dma((31,)), dma((31,)),
            dma((NZ - 1,)), dma((NZ - 1,)),
            dma((48,)), dma((48,)),
            dma((STEPS + 1,)), dma((STEPS + 1,)),
            dma((4,)),
        ],
        compiler_params=pltpu.CompilerParams(
            collective_id=0, has_side_effects=True, vmem_limit_bytes=40 * 1024 * 1024
        ),
    )(item_factors, user_start, tile_items, tile_seed, tile_count)


def solution(mesh):
    return jax.shard_map(
        on_device,
        mesh=mesh,
        in_specs=(
            P(("blk", "grp"), None),
            P("blk", None),
            P("blk", None),
            P("blk"),
            P("blk", None),
        ),
        out_specs=(P("blk", "grp"), P("blk", "grp")),
        check_vma=False,
    )
```
